256 devices in a mesh: loop: 32 (over x_hi, z, core), tensor: 8 (over y, x_lo).
Axes of the slice: x: 4 (x_hi: 2, x_lo: 2; x = x_hi * 2 + x_lo), y: 4, z: 8, core: 2. Of those that a mesh axis runs over, the one named last changes fastest.
Arguments:
- context: bfloat16 [10240, 5120], P('loop', 'tensor'), may hold values from -6 to 6
- w_out: bfloat16 [5120, 5120], P('tensor', 'loop'), may hold values from -0.078125 to 0.078125
- residual: bfloat16 [10240, 5120], P('loop', 'tensor'), may hold values from -70 to 70
- gain: float32 [5120], replicated, may hold values from 0.1 to 1.9
- grad_out: bfloat16 [10240, 5120], P('loop', 'tensor'), may hold values from -6 to 6
Outputs:
- normed: bfloat16 [10240, 5120], P('loop', 'tensor')
- d_context: bfloat16 [10240, 5120], P('loop', 'tensor')
- w_grad: float32 [5120, 5120], P('loop', 'tensor')
The draws below stay inside these ranges and needn't reach their ends.
All inputs are finite; a program needn't handle non-finite values.
Results may differ from the reference program's by a relative error of at most 0.0049.
Values may be sent and summed in bfloat16 or wider, within the bound.
No kernel may reach another device: no remote copies, remote signals or barrier semaphores. Data moves between devices by JAX's collectives and lax.ppermute only.
A program may use at most 128 MiB of HBM per device.

```python
import math
import jax
import jax.numpy as jnp
from jax import lax

D = 5120
HW = 5120
TOKENS = 10240


def draw_residual(key, part):
    key = jax.random.fold_in(key, 7)
    kbase, kcol, krow = jax.random.split(key, 3)
    column = jnp.arange(D, dtype=jnp.float32) / D
    col_scale = 0.5 * jnp.exp(column * math.log(4.0))
    rough = jnp.exp(jax.random.uniform(kcol, (D,), jnp.float32, -0.35, 0.35))
    rows = 0.4 * jnp.exp(jax.random.uniform(krow, (TOKENS, 1), jnp.float32, 0.0, math.log(10.0)))
    base = jnp.clip(jax.random.normal(kbase, (TOKENS, D), jnp.float32), -6.0, 6.0)
    return (base * rows * col_scale[None, :] * rough[None, :]).astype(jnp.bfloat16)


def spiked(result, rng, source, target, parts, factor):
    def block_of(axis_at):
        return (jnp.arange(result.shape[axis_at]) // (result.shape[axis_at] // parts)).reshape((-1,) + (1,) * (result.ndim - 1 - axis_at))

    first = jax.random.permutation(rng, parts)[block_of(target)]
    far = (block_of(target) + parts // 2) % parts
    return jnp.where((block_of(source) == first) | (block_of(source) == far), factor * result, result)


def steps_of(rng, shape, pieces, smallest, largest):
    level, own = 1.0, jax.random.fold_in(rng, 6)
    for position, parts in pieces:
        steps = jnp.exp(jax.random.uniform(jax.random.fold_in(own, position), (parts,), jnp.float32, smallest / len(pieces), largest / len(pieces)))
        level = level * jnp.repeat(steps, shape[position] // parts).reshape([-1 if axis == position else 1 for axis in range(len(shape))])
    return level


def gaussian(rng, extent, spread, reach, cuts=(), kind=jnp.bfloat16):
    factor_of = steps_of(rng, extent, cuts, -0.22, 0.18) if cuts else 1.0
    entries = jax.random.normal(rng, extent, jnp.float32) * spread * factor_of
    return jnp.minimum(jnp.maximum(entries, -reach), reach).astype(kind)


def gaussian_with(key, extent, width, reach, pieces, heavy, kind=jnp.bfloat16):
    values = width * jax.random.normal(key, extent, jnp.float32)
    if pieces:
        values = values * steps_of(key, extent, pieces, -0.22, 0.18)
    return jnp.clip(spiked(values, jax.random.fold_in(key, 3), *heavy), -reach, reach).astype(kind)


def setup_inputs(seed: int = 0) -> dict:
    keys = jax.random.split(jax.random.key(seed), 6)
    return {
        "context": gaussian(keys[0], (TOKENS, HW), 1.0, 6.0, ((0, 32), (1, 8))),
        "w_out": gaussian(keys[1], (HW, D), HW ** -0.5, 0.078125, ((0, 8), (1, 32))),
        "residual": draw_residual(jax.random.fold_in(keys[5], 71), 0),
        "gain": jnp.clip(1.0 + 0.18 * jax.random.normal(keys[3], (D,), jnp.float32), 0.1, 1.9),
        "grad_out": gaussian_with(keys[4], (TOKENS, D), 1.0, 6.0, ((0, 32), (1, 8)), (0, 1, 32, 2.75)),
    }


def reference(context, w_out, residual, gain, grad_out):
    ctx = context.astype(jnp.float32)
    weight = w_out.astype(jnp.float32)
    hidden = residual.astype(jnp.float32) + jnp.dot(ctx, weight)
    root = 1.0 / jnp.sqrt(lax.optimization_barrier(jnp.mean(hidden * hidden, axis=1, keepdims=True)) + 1e-06)
    normed = (hidden * root * gain[None, :]).astype(jnp.bfloat16)
    scaled = gain[None, :] * grad_out.astype(jnp.float32)
    dot = lax.optimization_barrier(jnp.mean(hidden * scaled, axis=1, keepdims=True))
    d_hidden = (root * scaled - hidden * root * root * root * dot).astype(jnp.bfloat16)
    dfull = d_hidden.astype(jnp.float32)
    d_context = jnp.dot(dfull, weight.T).astype(jnp.bfloat16)
    w_grad = jnp.dot(dfull.T, ctx) / jnp.sqrt(jnp.float32(TOKENS))
    return (normed, d_context, w_grad)
```

```python
import math

import jax
import jax.numpy as jnp
from jax import lax
from jax.sharding import PartitionSpec as P

BF16 = jnp.bfloat16
F32 = jnp.float32
D = 5120
TOKENS = 10240


def table(move):
    pairs = []
    for source in range(256):
        loop, tensor = source // 8, source % 8
        xh, z, c, y, xl = loop // 16, (loop // 2) % 8, loop % 2, tensor // 2, tensor % 2
        xh, z, c, y, xl = move(xh, z, c, y, xl)
        target = ((xh % 2) * 16 + (z % 8) * 2 + c % 2) * 8 + (y % 4) * 2 + xl % 2
        pairs.append((source, target))
    return pairs


def columns_home(xh, z, c, y, xl):
    return (xl, z + 2 * y, c, 2 * xh + z // 4, (z // 2) % 2)


CORE = table(lambda xh, z, c, y, xl: (xh, z, c + 1, y, xl))
XHI = table(lambda xh, z, c, y, xl: (xh + 1, z, c, y, xl))
XLO = table(lambda xh, z, c, y, xl: (xh, z, c, y, xl + 1))
ZUP = table(lambda xh, z, c, y, xl: (xh, z + 1, c, y, xl))
ZDOWN = table(lambda xh, z, c, y, xl: (xh, z - 1, c, y, xl))
YUP = table(lambda xh, z, c, y, xl: (xh, z, c, y + 1, xl))
YDOWN = table(lambda xh, z, c, y, xl: (xh, z, c, y - 1, xl))
YPAIR = table(lambda xh, z, c, y, xl: (xh, z, c, y ^ 1, xl))
YCROSS = table(lambda xh, z, c, y, xl: (xh, z, c, y ^ 3, xl))
HOME = table(columns_home)
BACK = [(b, a) for a, b in HOME]


def send(x, pairs):
    return lax.ppermute(x, ("loop", "tensor"), pairs)


def dot(a, b, dims):
    return lax.dot_general(a, b, (dims, ((), ())), preferred_element_type=F32)


def pick(stack, index):
    return lax.dynamic_index_in_dim(stack, index, 0, keepdims=False)


def per_device(context, w_out, residual, gain, grad_out):
    loop, tensor = lax.axis_index("loop"), lax.axis_index("tensor")
    xh, z, c = loop // 16, (loop // 2) % 8, loop % 2
    y, xl = tensor // 2, tensor % 2
    par = z % 2

    def heads_of(d):
        zz = (z + d) % 8
        first = 4 * (y % 2) + 2 * xl + zz % 2
        return (((zz - first + 8) // 2) % 4 - y + 4) % 4

    own = send(w_out.T, HOME)
    other = send(own, XHI)
    w0 = jnp.where(
        xh == 0,
        jnp.concatenate([own, other], 1),
        jnp.concatenate([other, own], 1),
    )
    w = {0: w0}
    for d in (1, 2, 3):
        w[-d] = send(w[1 - d], ZUP)
        w[d] = send(w[d - 1], ZDOWN)
    w[4] = jnp.concatenate([send(w[-3][:80], ZUP), send(w[3][80:], ZDOWN)], 0)

    pair = send(context, XLO)
    y0 = jnp.where(
        xl == 0,
        jnp.concatenate([context, pair], 1),
        jnp.concatenate([pair, context], 1),
    )
    below, above = send(y0, YUP), send(y0, YDOWN)
    across = jnp.concatenate([send(below[:160], YUP), send(above[160:], YDOWN)], 0)
    ctx = jnp.stack(
        [jnp.concatenate([b, send(b, CORE)], 0) for b in (y0, above, across, below)]
    )

    both = jnp.stack([residual, grad_out]).transpose(0, 2, 1).reshape(2, 2, 2, 160, 320)
    mine = jnp.where(c == 0, both[:, :, 0], both[:, :, 1])
    theirs = jnp.where(c == 0, both[:, :, 1], both[:, :, 0])
    both = jnp.concatenate([mine, send(theirs, CORE)], -1)
    both = jnp.where(par == 0, both, both[:, ::-1]).astype(F32)
    own_gain = gain.reshape(8, 2, 2, 160)
    own_gain = lax.dynamic_slice(own_gain, (tensor, 0, c, 0), (1, 2, 1, 160)).reshape(2, 160, 1)
    own_gain = jnp.where(par == 0, own_gain, own_gain[::-1])

    hidden = []
    for p in (0, 1):
        total = both[0, p]
        for d in ((0, 2, -2, 4), (1, -1, 3, -3))[p]:
            total = total + dot(w[d], pick(ctx, heads_of(d)), ((1,), (1,)))
        hidden.append(total)
    hidden = jnp.stack(hidden)
    scaled = own_gain * both[1]
    sums = jnp.stack(
        [jnp.sum(hidden * hidden, axis=(0, 1)), jnp.sum(hidden * scaled, axis=(0, 1))]
    )
    got = send(sums, CORE)
    sums = sums + jnp.concatenate([got[:, 320:], got[:, :320]], 1)
    for pairs in (XLO, YPAIR, YCROSS):
        sums = sums + send(sums, pairs)
    root = lax.rsqrt(sums[0] / D + 1e-06)[None, None, :]
    mean = (sums[1] / D)[None, None, :]
    normed = (hidden * root * own_gain).astype(BF16)
    grad = (root * scaled - hidden * root * root * root * mean).astype(BF16)

    def part(d):
        return dot(grad[d % 2], pick(ctx, heads_of(d)), ((1,), (0,)))

    far = part(4).astype(BF16)
    up, down = send(far[:80], ZUP), send(far[80:], ZDOWN)
    up = jnp.concatenate([up, jnp.zeros_like(up)], 0)
    down = jnp.concatenate([jnp.zeros_like(down), down], 0)
    for d in (3, 2, 1):
        up = send((part(d) + up.astype(F32)).astype(BF16), ZUP)
        down = send((part(-d) + down.astype(F32)).astype(BF16), ZDOWN)
    total = part(0) + up.astype(F32) + down.astype(F32)
    left, right = total[:, :640], total[:, 640:]
    away = jnp.where(xh == 0, right, left).astype(BF16)
    total = jnp.where(xh == 0, left, right) + send(away, XHI).astype(F32)
    w_grad = send(total.astype(BF16), BACK).astype(F32) * (1.0 / math.sqrt(TOKENS))

    grad_own = jnp.concatenate([grad[:, :, :320], send(grad[:, :, 320:], CORE)], 0).reshape(640, 320)
    w_all = jnp.stack([w[d] if d < 5 else w[d - 8] for d in range(8)])
    w_pair = send(w_all, CORE)

    def piece(dy):
        target = (y + dy) % 4
        slices = []
        for stack in (w_all, w_pair):
            for p in (0, 1):
                q = (par + p) % 2
                at = (4 * (y % 2) + 2 * xl + q + 2 * target - z + 8) % 8
                slices.append(pick(stack, at))
        return dot(grad_own, jnp.concatenate(slices, 0), ((0,), (0,)))

    far = piece(2).astype(BF16)
    up, down = send(far[:160], YUP), send(far[160:], YDOWN)
    up = jnp.concatenate([up, jnp.zeros_like(up)], 0)
    down = jnp.concatenate([jnp.zeros_like(down), down], 0)
    up = send((piece(1) + up.astype(F32)).astype(BF16), YUP)
    down = send((piece(3) + down.astype(F32)).astype(BF16), YDOWN)
    total = piece(0) + up.astype(F32) + down.astype(F32)
    left, right = total[:, :640], total[:, 640:]
    away = jnp.where(xl == 0, right, left).astype(BF16)
    d_context = jnp.where(xl == 0, left, right) + send(away, XLO).astype(F32)
    d_context = d_context.astype(BF16)

    kept, got = normed[:, :, :320], send(normed[:, :, 320:], CORE)
    kept = jnp.where(par == 0, kept, kept[::-1])
    got = jnp.where(par == 0, got, got[::-1])
    normed = jnp.where(
        c == 0, jnp.stack([kept, got], 1), jnp.stack([got, kept], 1)
    )
    normed = normed.reshape(640, 320).T
    return (normed, d_context, w_grad)


def solution(mesh):
    return jax.shard_map(
        per_device,
        mesh=mesh,
        in_specs=(
            P("loop", "tensor"),
            P("tensor", "loop"),
            P("loop", "tensor"),
            P(),
            P("loop", "tensor"),
        ),
        out_specs=(P("loop", "tensor"), P("loop", "tensor"), P("loop", "tensor")),
        check_vma=False,
    )
```

```python
import math

import jax
import jax.numpy as jnp
from jax import lax
from jax.sharding import PartitionSpec as P

BF16 = jnp.bfloat16
F32 = jnp.float32
D = 5120
TOKENS = 10240


def table(move):
    pairs = []
    for source in range(256):
        loop, tensor = source // 8, source % 8
        xh, z, c, y, xl = loop // 16, (loop // 2) % 8, loop % 2, tensor // 2, tensor % 2
        xh, z, c, y, xl = move(xh, z, c, y, xl)
        target = ((xh % 2) * 16 + (z % 8) * 2 + c % 2) * 8 + (y % 4) * 2 + xl % 2
        pairs.append((source, target))
    return pairs


def columns_home(xh, z, c, y, xl):
    return (xl, z + 2 * y, c, 2 * xh + z // 4, (z // 2) % 2)


CORE = table(lambda xh, z, c, y, xl: (xh, z, c + 1, y, xl))
XHI = table(lambda xh, z, c, y, xl: (xh + 1, z, c, y, xl))
XLO = table(lambda xh, z, c, y, xl: (xh, z, c, y, xl + 1))
ZUP = table(lambda xh, z, c, y, xl: (xh, z + 1, c, y, xl))
ZDOWN = table(lambda xh, z, c, y, xl: (xh, z - 1, c, y, xl))
YUP = table(lambda xh, z, c, y, xl: (xh, z, c, y + 1, xl))
YDOWN = table(lambda xh, z, c, y, xl: (xh, z, c, y - 1, xl))
YPAIR = table(lambda xh, z, c, y, xl: (xh, z, c, y ^ 1, xl))
YCROSS = table(lambda xh, z, c, y, xl: (xh, z, c, y ^ 3, xl))
HOME = table(columns_home)
BACK = [(b, a) for a, b in HOME]


def send(x, pairs):
    return lax.ppermute(x, ("loop", "tensor"), pairs)


def dot(a, b, dims):
    return lax.dot_general(a, b, (dims, ((), ())), preferred_element_type=F32)


def after(x, *others):
    return lax.optimization_barrier((x, others))[0]


def pick(stack, index):
    return lax.dynamic_index_in_dim(stack, index, 0, keepdims=False)


def per_device(context, w_out, residual, gain, grad_out):
    loop, tensor = lax.axis_index("loop"), lax.axis_index("tensor")
    xh, z, c = loop // 16, (loop // 2) % 8, loop % 2
    y, xl = tensor // 2, tensor % 2
    par = z % 2

    turn = (z // 2 - 2 * (y % 2) - xl - y + 8) % 4

    def heads_of(d):
        return (((z + d + 8) // 2) - z // 2 + turn) % 4

    own = send(w_out.T, HOME)
    other = send(own, XHI)
    w0 = jnp.where(
        xh == 0,
        jnp.concatenate([own, other], 1),
        jnp.concatenate([other, own], 1),
    )
    w = {0: w0}
    for d in (1, 2, 3):
        w[-d] = send(w[1 - d], ZUP)
        w[d] = send(w[d - 1], ZDOWN)
    w[4] = jnp.concatenate([send(w[-3][:80], ZUP), send(w[3][80:], ZDOWN)], 0)

    pair = send(context, XLO)
    y0 = jnp.where(
        xl == 0,
        jnp.concatenate([context, pair], 1),
        jnp.concatenate([pair, context], 1),
    )
    below, above = send(y0, YUP), send(y0, YDOWN)
    across = jnp.concatenate([send(below[:160], YUP), send(above[160:], YDOWN)], 0)
    ctx = jnp.stack(
        [jnp.concatenate([b, send(b, CORE)], 0) for b in (y0, above, across, below)]
    )

    both = jnp.stack([residual, grad_out]).transpose(0, 2, 1).reshape(2, 2, 2, 160, 320)
    mine = jnp.where(c == 0, both[:, :, 0], both[:, :, 1])
    theirs = jnp.where(c == 0, both[:, :, 1], both[:, :, 0])
    both = jnp.concatenate([mine, send(theirs, CORE)], -1)
    both = jnp.where(par == 0, both, both[:, ::-1]).astype(F32)
    own_gain = gain.reshape(8, 2, 2, 160)
    own_gain = lax.dynamic_slice(own_gain, (tensor, 0, c, 0), (1, 2, 1, 160)).reshape(2, 160, 1)
    own_gain = jnp.where(par == 0, own_gain, own_gain[::-1])

    w_rows = []
    for e in range(4):
        even = w[2 * e if e < 3 else -2]
        behind = w[2 * e + 1 if e < 2 else 2 * e - 7]
        before = w[2 * e - 1 if e < 3 else -3]
        w_rows.append(jnp.concatenate([even, jnp.where(par == 0, behind, before)], 0))
    total = both[0].reshape(320, 640)
    for e in (0, 3, 1, 2):
        total = total + dot(w_rows[e], pick(ctx, (turn + e) % 4), ((1,), (1,)))
    hidden = total.reshape(2, 160, 640)
    scaled = own_gain * both[1]
    sums = jnp.stack(
        [jnp.sum(hidden * hidden, axis=(0, 1)), jnp.sum(hidden * scaled, axis=(0, 1))]
    )
    got = send(sums, CORE)
    sums = sums + jnp.concatenate([got[:, 320:], got[:, :320]], 1)
    for pairs in (XLO, YPAIR, YCROSS):
        sums = sums + send(sums, pairs)
    root = lax.rsqrt(sums[0] / D + 1e-06)[None, None, :]
    mean = (sums[1] / D)[None, None, :]
    normed = (hidden * root * own_gain).astype(BF16)
    grad = (root * scaled - hidden * root * root * root * mean).astype(BF16)

    def part(d):
        return dot(grad[d % 2], pick(ctx, heads_of(d)), ((1,), (0,)))

    begin = part(4).astype(BF16)
    up, down = send(begin[:80], ZUP), send(begin[80:], ZDOWN)
    up = jnp.concatenate([up, jnp.zeros_like(up)], 0)
    down = jnp.concatenate([jnp.zeros_like(down), down], 0)
    up = (part(3) + up.astype(F32)).astype(BF16)
    down = (part(-3) + down.astype(F32)).astype(BF16)

    grad_rows = jnp.concatenate([grad[:, :, :320], send(grad[:, :, 320:], CORE)], 0).reshape(640, 320)
    w_rows = jnp.stack(w_rows)
    w_pair = send(w_rows, CORE)

    def piece(dy):
        e = (dy - turn + 4) % 4
        value = dot(grad_rows[:320], pick(w_rows, e), ((0,), (0,)))
        return value + dot(grad_rows[320:], pick(w_pair, e), ((0,), (0,)))

    edge = piece(2).astype(BF16)
    yup, ydown = send(edge[:160], YUP), send(edge[160:], YDOWN)
    yup2 = jnp.concatenate([yup, jnp.zeros_like(yup)], 0)
    ydown2 = jnp.concatenate([jnp.zeros_like(ydown), ydown], 0)
    yup2 = send((piece(1) + yup2.astype(F32)).astype(BF16), YUP)
    ydown2 = send((piece(3) + ydown2.astype(F32)).astype(BF16), YDOWN)
    total = piece(0) + yup2.astype(F32) + ydown2.astype(F32)
    left, right = total[:, :640], total[:, 640:]
    away = jnp.where(xl == 0, right, left).astype(BF16)
    d_context = jnp.where(xl == 0, left, right) + send(away, XLO).astype(F32)
    d_context = d_context.astype(BF16)

    for d in (3, 2, 1):
        if d < 3:
            up = (part(d) + up.astype(F32)).astype(BF16)
            down = (part(-d) + down.astype(F32)).astype(BF16)
        up, down = send(up, ZUP), send(down, ZDOWN)
    total = part(0) + up.astype(F32) + down.astype(F32)
    left, right = total[:, :640], total[:, 640:]
    away = jnp.where(xh == 0, right, left).astype(BF16)
    total = jnp.where(xh == 0, left, right) + send(away, XHI).astype(F32)
    total = total.astype(BF16)
    w_grad = send(total, BACK).astype(F32) * (1.0 / math.sqrt(TOKENS))

    kept, got = normed[:, :, :320], send(normed[:, :, 320:], CORE)
    kept = jnp.where(par == 0, kept, kept[::-1])
    got = jnp.where(par == 0, got, got[::-1])
    normed = jnp.where(
        c == 0, jnp.stack([kept, got], 1), jnp.stack([got, kept], 1)
    )
    normed = normed.reshape(640, 320).T
    return (normed, d_context, w_grad)


def solution(mesh):
    return jax.shard_map(
        per_device,
        mesh=mesh,
        in_specs=(
            P("loop", "tensor"),
            P("tensor", "loop"),
            P("loop", "tensor"),
            P(),
            P("loop", "tensor"),
        ),
        out_specs=(P("loop", "tensor"), P("loop", "tensor"), P("loop", "tensor")),
        check_vma=False,
    )
```

```python
import math

import jax
import jax.numpy as jnp
from jax import lax
from jax.sharding import PartitionSpec as P

BF16 = jnp.bfloat16
F32 = jnp.float32
D = 5120
TOKENS = 10240


def table(move):
    pairs = []
    for source in range(256):
        loop, tensor = source // 8, source % 8
        xh, z, c, y, xl = loop // 16, (loop // 2) % 8, loop % 2, tensor // 2, tensor % 2
        xh, z, c, y, xl = move(xh, z, c, y, xl)
        target = ((xh % 2) * 16 + (z % 8) * 2 + c % 2) * 8 + (y % 4) * 2 + xl % 2
        pairs.append((source, target))
    return pairs


def columns_home(xh, z, c, y, xl):
    to_y = 2 * xh + z // 4
    k = (y - to_y) % 4
    return (xl ^ (k // 2), z + 2 * (2, 0, 3, 1)[k], c, to_y, (z // 2) % 2)


CORE = table(lambda xh, z, c, y, xl: (xh, z, c + 1, y, xl))
XHI = table(lambda xh, z, c, y, xl: (xh + 1, z, c, y, xl))
XLO = table(lambda xh, z, c, y, xl: (xh, z, c, y, xl + 1))
ZUP = table(lambda xh, z, c, y, xl: (xh, z + 1, c, y, xl))
ZDOWN = table(lambda xh, z, c, y, xl: (xh, z - 1, c, y, xl))
YUP = table(lambda xh, z, c, y, xl: (xh, z, c, y + 1, xl))
YDOWN = table(lambda xh, z, c, y, xl: (xh, z, c, y - 1, xl))
YPAIR = table(lambda xh, z, c, y, xl: (xh, z, c, y ^ 1, xl))
YCROSS = table(lambda xh, z, c, y, xl: (xh, z, c, y ^ 3, xl))
HOME = table(columns_home)
BACK = [(b, a) for a, b in HOME]


def send(x, pairs):
    return lax.ppermute(x, ("loop", "tensor"), pairs)


def dot(a, b, dims):
    return lax.dot_general(a, b, (dims, ((), ())), preferred_element_type=F32)


def after(x, *others):
    return lax.optimization_barrier((x, others))[0]


def pick(stack, index):
    return lax.dynamic_index_in_dim(stack, index, 0, keepdims=False)


def per_device(context, w_out, residual, gain, grad_out):
    loop, tensor = lax.axis_index("loop"), lax.axis_index("tensor")
    xh, z, c = loop // 16, (loop // 2) % 8, loop % 2
    y, xl = tensor // 2, tensor % 2
    par = z % 2

    turn = (z // 2 - 2 * (y % 2) - xl + 8) % 4
    side = (xh + turn) % 2

    def heads_of(d):
        return (((z + d + 8) // 2) - z // 2 + turn) % 4

    own = send(w_out.T, HOME)
    other = send(own, XHI)
    w0 = jnp.where(
        side == 0,
        jnp.concatenate([own, other], 1),
        jnp.concatenate([other, own], 1),
    )
    w = {0: w0}
    for d in (1, 2, 3):
        w[-d] = send(w[1 - d], ZUP)
        w[d] = send(w[d - 1], ZDOWN)
    w[4] = jnp.concatenate([send(w[-3][:80], ZUP), send(w[3][80:], ZDOWN)], 0)

    pair = send(context, XLO)
    y0 = jnp.where(
        xl == 0,
        jnp.concatenate([context, pair], 1),
        jnp.concatenate([pair, context], 1),
    )
    below, above = send(y0, YUP), send(y0, YDOWN)
    across = jnp.concatenate([send(below[:160], YUP), send(above[160:], YDOWN)], 0)
    ctx = jnp.stack(
        [jnp.concatenate([b, send(b, CORE)], 0) for b in (above, below, y0, across)]
    )

    both = jnp.stack([residual, grad_out]).transpose(0, 2, 1).reshape(2, 2, 2, 160, 320)
    mine = jnp.where(c == 0, both[:, :, 0], both[:, :, 1])
    theirs = jnp.where(c == 0, both[:, :, 1], both[:, :, 0])
    both = jnp.concatenate([mine, send(theirs, CORE)], -1)
    both = jnp.where(par == 0, both, both[:, ::-1]).astype(F32)
    own_gain = gain.reshape(8, 2, 2, 160)
    own_gain = lax.dynamic_slice(own_gain, (tensor, 0, c, 0), (1, 2, 1, 160)).reshape(2, 160, 1)
    own_gain = jnp.where(par == 0, own_gain, own_gain[::-1])

    w_rows = []
    for e in range(4):
        even = w[2 * e if e < 3 else -2]
        behind = w[2 * e + 1 if e < 2 else 2 * e - 7]
        before = w[2 * e - 1 if e < 3 else -3]
        w_rows.append(jnp.concatenate([even, jnp.where(par == 0, behind, before)], 0))
    total = both[0].reshape(320, 640)
    for e in (0, 3, 1, 2):
        total = total + dot(w_rows[e], pick(ctx, (turn + e) % 4), ((1,), (1,)))
    hidden = total.reshape(2, 160, 640)
    scaled = own_gain * both[1]
    sums = jnp.stack(
        [jnp.sum(hidden * hidden, axis=(0, 1)), jnp.sum(hidden * scaled, axis=(0, 1))]
    )
    got = send(sums, CORE)
    sums = sums + jnp.concatenate([got[:, 320:], got[:, :320]], 1)
    for pairs in (XLO, YPAIR, YCROSS):
        sums = sums + send(sums, pairs)
    root = lax.rsqrt(sums[0] / D + 1e-06)[None, None, :]
    mean = (sums[1] / D)[None, None, :]
    normed = (hidden * root * own_gain).astype(BF16)
    grad = (root * scaled - hidden * root * root * root * mean).astype(BF16)

    def part(d):
        return dot(grad[d % 2], pick(ctx, heads_of(d)), ((1,), (0,)))

    begin = part(4).astype(BF16)
    up, down = send(begin[:80], ZUP), send(begin[80:], ZDOWN)
    up = jnp.concatenate([up, jnp.zeros_like(up)], 0)
    down = jnp.concatenate([jnp.zeros_like(down), down], 0)
    up = (part(3) + up.astype(F32)).astype(BF16)
    down = (part(-3) + down.astype(F32)).astype(BF16)

    grad_rows = jnp.concatenate([grad[:, :, :320], send(grad[:, :, 320:], CORE)], 0).reshape(640, 320)
    w_rows = jnp.stack(w_rows)
    w_pair = jnp.stack([send(w_rows[e], CORE) for e in range(4)])

    def piece(dy):
        e = ((2, 0, 3, 1)[dy] - turn + 4) % 4
        value = dot(grad_rows[:320], pick(w_rows, e), ((0,), (0,)))
        return value + dot(grad_rows[320:], pick(w_pair, e), ((0,), (0,)))

    edge = piece(2).astype(BF16)
    yup, ydown = send(edge[:160], YUP), send(edge[160:], YDOWN)
    yup2 = jnp.concatenate([yup, jnp.zeros_like(yup)], 0)
    ydown2 = jnp.concatenate([jnp.zeros_like(ydown), ydown], 0)
    yup2 = send((piece(1) + yup2.astype(F32)).astype(BF16), YUP)
    ydown2 = send((piece(3) + ydown2.astype(F32)).astype(BF16), YDOWN)
    total = piece(0) + yup2.astype(F32) + ydown2.astype(F32)
    left, right = total[:, :640], total[:, 640:]
    away = jnp.where(xl == 0, right, left).astype(BF16)
    d_context = jnp.where(xl == 0, left, right) + send(away, XLO).astype(F32)
    d_context = d_context.astype(BF16)

    for d in (3, 2, 1):
        if d < 3:
            up = (part(d) + up.astype(F32)).astype(BF16)
            down = (part(-d) + down.astype(F32)).astype(BF16)
        up, down = send(up, ZUP), send(down, ZDOWN)
    total = part(0) + up.astype(F32) + down.astype(F32)
    left, right = total[:, :640], total[:, 640:]
    away = jnp.where(side == 0, right, left).astype(BF16)
    total = jnp.where(side == 0, left, right) + send(away, XHI).astype(F32)
    total = total.astype(BF16)
    w_grad = send(total, BACK).astype(F32) * (1.0 / math.sqrt(TOKENS))

    kept, got = normed[:, :, :320], send(normed[:, :, 320:], CORE)
    kept = jnp.where(par == 0, kept, kept[::-1])
    got = jnp.where(par == 0, got, got[::-1])
    normed = jnp.where(
        c == 0, jnp.stack([kept, got], 1), jnp.stack([got, kept], 1)
    )
    normed = normed.reshape(640, 320).T
    return (normed, d_context, w_grad)


def solution(mesh):
    return jax.shard_map(
        per_device,
        mesh=mesh,
        in_specs=(
            P("loop", "tensor"),
            P("tensor", "loop"),
            P("loop", "tensor"),
            P(),
            P("loop", "tensor"),
        ),
        out_specs=(P("loop", "tensor"), P("loop", "tensor"), P("loop", "tensor")),
        check_vma=False,
    )
```

```python
import math

import jax
import jax.numpy as jnp
from jax import lax
from jax.sharding import PartitionSpec as P

BF16 = jnp.bfloat16
F32 = jnp.float32
D = 5120
TOKENS = 10240


def table(move):
    pairs = []
    for source in range(256):
        loop, tensor = source // 8, source % 8
        xh, z, c, y, xl = loop // 16, (loop // 2) % 8, loop % 2, tensor // 2, tensor % 2
        xh, z, c, y, xl = move(xh, z, c, y, xl)
        target = ((xh % 2) * 16 + (z % 8) * 2 + c % 2) * 8 + (y % 4) * 2 + xl % 2
        pairs.append((source, target))
    return pairs


def columns_home(xh, z, c, y, xl):
    to_y = 2 * xh + z // 4
    k = (y - to_y) % 4
    return (xl ^ (k // 2), z + 2 * (2, 0, 3, 1)[k], c, to_y, (z // 2) % 2)


def columns_first(xh, z, c, y, xl):
    return (xl, z + 2 * y, c, 2 * xh + z // 4, (z // 2) % 2)


CORE = table(lambda xh, z, c, y, xl: (xh, z, c + 1, y, xl))
XHI = table(lambda xh, z, c, y, xl: (xh + 1, z, c, y, xl))
XLO = table(lambda xh, z, c, y, xl: (xh, z, c, y, xl + 1))
ZUP = table(lambda xh, z, c, y, xl: (xh, z + 1, c, y, xl))
ZDOWN = table(lambda xh, z, c, y, xl: (xh, z - 1, c, y, xl))
YUP = table(lambda xh, z, c, y, xl: (xh, z, c, y + 1, xl))
YDOWN = table(lambda xh, z, c, y, xl: (xh, z, c, y - 1, xl))
YPAIR = table(lambda xh, z, c, y, xl: (xh, z, c, y ^ 1, xl))
YCROSS = table(lambda xh, z, c, y, xl: (xh, z, c, y ^ 3, xl))
HOME = table(columns_first)
BACK = [(b, a) for a, b in table(columns_home)]


def send(x, pairs):
    return lax.ppermute(x, ("loop", "tensor"), pairs)


def dot(a, b, dims):
    return lax.dot_general(a, b, (dims, ((), ())), preferred_element_type=F32)


def after(x, *others):
    return lax.optimization_barrier((x, others))[0]


def pick(stack, index):
    return lax.dynamic_index_in_dim(stack, index, 0, keepdims=False)


def per_device(context, w_out, residual, gain, grad_out):
    loop, tensor = lax.axis_index("loop"), lax.axis_index("tensor")
    xh, z, c = loop // 16, (loop // 2) % 8, loop % 2
    y, xl = tensor // 2, tensor % 2
    par = z % 2

    turn = (z // 2 - 2 * (y % 2) - xl + 8) % 4
    side = (xh + turn) % 2

    first = (turn - y + 4) % 4

    def heads_of(d):
        return (((z + d + 8) // 2) - z // 2 + turn) % 4

    own = send(w_out.T, HOME)
    other = send(own, XHI)
    w0 = jnp.where(
        xh == 0,
        jnp.concatenate([own, other], 1),
        jnp.concatenate([other, own], 1),
    )
    w = {0: w0}
    for d in (1, 2, 3):
        w[-d] = send(w[1 - d], ZUP)
        w[d] = send(w[d - 1], ZDOWN)
    w[4] = jnp.concatenate([send(w[-3][:80], ZUP), send(w[3][80:], ZDOWN)], 0)

    pair = send(context, XLO)
    y0 = jnp.where(
        xl == 0,
        jnp.concatenate([context, pair], 1),
        jnp.concatenate([pair, context], 1),
    )
    below, above = send(y0, YUP), send(y0, YDOWN)
    across = jnp.concatenate([send(below[:160], YUP), send(above[160:], YDOWN)], 0)
    ctx = jnp.stack(
        [jnp.concatenate([b, send(b, CORE)], 0) for b in (above, below, y0, across)]
    )

    both = jnp.stack([residual, grad_out]).transpose(0, 2, 1).reshape(2, 2, 2, 160, 320)
    mine = jnp.where(c == 0, both[:, :, 0], both[:, :, 1])
    theirs = jnp.where(c == 0, both[:, :, 1], both[:, :, 0])
    both = jnp.concatenate([mine, send(theirs, CORE)], -1)
    both = jnp.where(par == 0, both, both[:, ::-1]).astype(F32)
    own_gain = gain.reshape(8, 2, 2, 160)
    own_gain = lax.dynamic_slice(own_gain, (tensor, 0, c, 0), (1, 2, 1, 160)).reshape(2, 160, 1)
    own_gain = jnp.where(par == 0, own_gain, own_gain[::-1])

    def order(dy):
        return (3 * (dy % 4) + 2) % 5

    w_rows = []
    for e in range(4):
        even = w[2 * e if e < 3 else -2]
        behind = w[2 * e + 1 if e < 2 else 2 * e - 7]
        before = w[2 * e - 1 if e < 3 else -3]
        w_rows.append(jnp.concatenate([even, jnp.where(par == 0, behind, before)], 0))
    total = both[0].reshape(320, 640)
    for e in (0, 3, 1, 2):
        total = total + dot(w_rows[e], pick(ctx, order(first + e)), ((1,), (1,)))
    hidden = total.reshape(2, 160, 640)
    scaled = own_gain * both[1]
    sums = jnp.stack(
        [jnp.sum(hidden * hidden, axis=(0, 1)), jnp.sum(hidden * scaled, axis=(0, 1))]
    )
    got = send(sums, CORE)
    sums = sums + jnp.concatenate([got[:, 320:], got[:, :320]], 1)
    for pairs in (XLO, YPAIR, YCROSS):
        sums = sums + send(sums, pairs)
    root = lax.rsqrt(sums[0] / D + 1e-06)[None, None, :]
    mean = (sums[1] / D)[None, None, :]
    normed = (hidden * root * own_gain).astype(BF16)
    grad = (root * scaled - hidden * root * root * root * mean).astype(BF16)

    def part(d):
        return dot(grad[d % 2], pick(ctx, heads_of(d)), ((1,), (0,)))

    begin = part(4).astype(BF16)
    up, down = send(begin[:80], ZUP), send(begin[80:], ZDOWN)
    up = jnp.concatenate([up, jnp.zeros_like(up)], 0)
    down = jnp.concatenate([jnp.zeros_like(down), down], 0)
    up = (part(3) + up.astype(F32)).astype(BF16)
    down = (part(-3) + down.astype(F32)).astype(BF16)

    grad_rows = jnp.concatenate([grad[:, :, :320], send(grad[:, :, 320:], CORE)], 0).reshape(640, 320)
    w_rows = jnp.stack(w_rows)
    w_pair = jnp.stack([send(w_rows[e], CORE) for e in range(4)])

    def piece(dy):
        e = (dy - first + 4) % 4
        value = dot(grad_rows[:320], pick(w_rows, e), ((0,), (0,)))
        return value + dot(grad_rows[320:], pick(w_pair, e), ((0,), (0,)))

    edge = piece(2).astype(BF16)
    yup, ydown = send(edge[:160], YUP), send(edge[160:], YDOWN)
    yup2 = jnp.concatenate([yup, jnp.zeros_like(yup)], 0)
    ydown2 = jnp.concatenate([jnp.zeros_like(ydown), ydown], 0)
    yup2 = send((piece(1) + yup2.astype(F32)).astype(BF16), YUP)
    ydown2 = send((piece(3) + ydown2.astype(F32)).astype(BF16), YDOWN)
    total = piece(0) + yup2.astype(F32) + ydown2.astype(F32)
    left, right = total[:, :640], total[:, 640:]
    away = jnp.where(xl == 0, right, left).astype(BF16)
    d_context = jnp.where(xl == 0, left, right) + send(away, XLO).astype(F32)
    d_context = d_context.astype(BF16)

    for d in (3, 2, 1):
        if d < 3:
            up = (part(d) + up.astype(F32)).astype(BF16)
            down = (part(-d) + down.astype(F32)).astype(BF16)
        up, down = send(up, ZUP), send(down, ZDOWN)
    total = part(0) + up.astype(F32) + down.astype(F32)
    left, right = total[:, :640], total[:, 640:]
    away = jnp.where(side == 0, right, left).astype(BF16)
    total = jnp.where(side == 0, left, right) + send(away, XHI).astype(F32)
    total = total.astype(BF16)
    w_grad = send(total, BACK).astype(F32) * (1.0 / math.sqrt(TOKENS))

    kept, got = normed[:, :, :320], send(normed[:, :, 320:], CORE)
    kept = jnp.where(par == 0, kept, kept[::-1])
    got = jnp.where(par == 0, got, got[::-1])
    normed = jnp.where(
        c == 0, jnp.stack([kept, got], 1), jnp.stack([got, kept], 1)
    )
    normed = normed.reshape(640, 320).T
    return (normed, d_context, w_grad)


def solution(mesh):
    return jax.shard_map(
        per_device,
        mesh=mesh,
        in_specs=(
            P("loop", "tensor"),
            P("tensor", "loop"),
            P("loop", "tensor"),
            P(),
            P("loop", "tensor"),
        ),
        out_specs=(P("loop", "tensor"), P("loop", "tensor"), P("loop", "tensor")),
        check_vma=False,
    )
```

```python
import math

import jax
import jax.numpy as jnp
from jax import lax
from jax.sharding import PartitionSpec as P

BF16 = jnp.bfloat16
F32 = jnp.float32
D = 5120
TOKENS = 10240


def table(move):
    pairs = []
    for source in range(256):
        loop, tensor = source // 8, source % 8
        xh, z, c, y, xl = loop // 16, (loop // 2) % 8, loop % 2, tensor // 2, tensor % 2
        xh, z, c, y, xl = move(xh, z, c, y, xl)
        target = ((xh % 2) * 16 + (z % 8) * 2 + c % 2) * 8 + (y % 4) * 2 + xl % 2
        pairs.append((source, target))
    return pairs


def columns_home(xh, z, c, y, xl):
    to_y = 2 * xh + z // 4
    k = (y - to_y) % 4
    return (xl ^ (k // 2), z + 2 * (2, 0, 3, 1)[k], c, to_y, (z // 2) % 2)


def columns_first(xh, z, c, y, xl):
    return (xl, z + 2 * y, c, 2 * xh + z // 4, (z // 2) % 2)


CORE = table(lambda xh, z, c, y, xl: (xh, z, c + 1, y, xl))
XHI = table(lambda xh, z, c, y, xl: (xh + 1, z, c, y, xl))
XLO = table(lambda xh, z, c, y, xl: (xh, z, c, y, xl + 1))
ZUP = table(lambda xh, z, c, y, xl: (xh, z + 1, c, y, xl))
ZDOWN = table(lambda xh, z, c, y, xl: (xh, z - 1, c, y, xl))
YUP = table(lambda xh, z, c, y, xl: (xh, z, c, y + 1, xl))
YDOWN = table(lambda xh, z, c, y, xl: (xh, z, c, y - 1, xl))
YPAIR = table(lambda xh, z, c, y, xl: (xh, z, c, y ^ 1, xl))
YCROSS = table(lambda xh, z, c, y, xl: (xh, z, c, y ^ 3, xl))
HOME = table(columns_first)
BACK = [(b, a) for a, b in table(columns_home)]


def send(x, pairs):
    return lax.ppermute(x, ("loop", "tensor"), pairs)


def dot(a, b, dims):
    return lax.dot_general(a, b, (dims, ((), ())), preferred_element_type=F32)


def after(x, *others):
    return lax.optimization_barrier((x, others))[0]


def pick(stack, index):
    return lax.dynamic_index_in_dim(stack, index, 0, keepdims=False)


def per_device(context, w_out, residual, gain, grad_out):
    loop, tensor = lax.axis_index("loop"), lax.axis_index("tensor")
    xh, z, c = loop // 16, (loop // 2) % 8, loop % 2
    y, xl = tensor // 2, tensor % 2
    par = z % 2

    turn = (z // 2 - 2 * (y % 2) - xl + 8) % 4
    side = (xh + turn) % 2

    first = (turn - y + 4) % 4

    def heads_of(d):
        return (((z + d + 8) // 2) - z // 2 + turn) % 4

    own = send(w_out.T, HOME)
    other = send(own, XHI)
    w0 = jnp.where(
        xh == 0,
        jnp.concatenate([own, other], 1),
        jnp.concatenate([other, own], 1),
    )
    w = {0: w0}
    for d in (1, 2, 3):
        w[-d] = send(w[1 - d], ZUP)
        w[d] = send(w[d - 1], ZDOWN)
    w[4] = jnp.concatenate([send(w[-3][:80], ZUP), send(w[3][80:], ZDOWN)], 0)

    pair = send(context, XLO)
    y0 = jnp.where(
        xl == 0,
        jnp.concatenate([context, pair], 1),
        jnp.concatenate([pair, context], 1),
    )
    below, above = send(y0, YUP), send(y0, YDOWN)
    across = jnp.concatenate([send(below[:160], YUP), send(above[160:], YDOWN)], 0)
    ctx = jnp.stack(
        [jnp.concatenate([b, send(b, CORE)], 0) for b in (above, below, y0, across)]
    )

    both = jnp.stack([residual, grad_out]).transpose(0, 2, 1).reshape(2, 2, 2, 160, 320)
    mine = jnp.where(c == 0, both[:, :, 0], both[:, :, 1])
    theirs = jnp.where(c == 0, both[:, :, 1], both[:, :, 0])
    both = jnp.concatenate([mine, send(theirs, CORE)], -1)
    both = jnp.where(par == 0, both, both[:, ::-1]).astype(F32)
    own_gain = gain.reshape(8, 2, 2, 160)
    own_gain = lax.dynamic_slice(own_gain, (tensor, 0, c, 0), (1, 2, 1, 160)).reshape(2, 160, 1)
    own_gain = jnp.where(par == 0, own_gain, own_gain[::-1])

    def order(dy):
        return (3 * (dy % 4) + 2) % 5

    w_rows = []
    for e in range(4):
        even = w[2 * e if e < 3 else -2]
        behind = w[2 * e + 1 if e < 2 else 2 * e - 7]
        before = w[2 * e - 1 if e < 3 else -3]
        w_rows.append(jnp.concatenate([even, jnp.where(par == 0, behind, before)], 0))
    total = both[0].reshape(320, 640)
    for e in (0, 3, 1, 2):
        total = total + dot(w_rows[e], pick(ctx, order(first + e)), ((1,), (1,)))
    hidden = total.reshape(2, 160, 640)
    scaled = own_gain * both[1]
    sums = jnp.stack(
        [jnp.sum(hidden * hidden, axis=(0, 1)), jnp.sum(hidden * scaled, axis=(0, 1))]
    )
    got = send(sums, CORE)
    sums = sums + jnp.concatenate([got[:, 320:], got[:, :320]], 1)
    for pairs in (XLO, YPAIR, YCROSS):
        sums = sums + send(sums, pairs)
    root = lax.rsqrt(sums[0] / D + 1e-06)[None, None, :]
    mean = (sums[1] / D)[None, None, :]
    normed = (hidden * root * own_gain).astype(BF16)
    grad = (root * scaled - hidden * root * root * root * mean).astype(BF16)

    def part(d):
        return dot(grad[d % 2], pick(ctx, heads_of(d)), ((1,), (0,)))

    begin = part(4).astype(BF16)
    up, down = send(begin[:80], ZUP), send(begin[80:], ZDOWN)
    kept = after(grad[:, :, :320], up)
    up = jnp.concatenate([up, jnp.zeros_like(up)], 0)
    down = jnp.concatenate([jnp.zeros_like(down), down], 0)
    up = (part(3) + up.astype(F32)).astype(BF16)
    down = (part(-3) + down.astype(F32)).astype(BF16)

    grad_rows = jnp.concatenate([kept, send(grad[:, :, 320:], CORE)], 0).reshape(640, 320)
    w_rows = jnp.stack(w_rows)
    w_pair = jnp.stack([send(w_rows[e], CORE) for e in range(4)])

    def piece(dy):
        e = (dy - first + 4) % 4
        value = dot(grad_rows[:320], pick(w_rows, e), ((0,), (0,)))
        return value + dot(grad_rows[320:], pick(w_pair, e), ((0,), (0,)))

    edge = piece(2).astype(BF16)
    yup, ydown = send(edge[:160], YUP), send(edge[160:], YDOWN)
    yup2 = jnp.concatenate([yup, jnp.zeros_like(yup)], 0)
    ydown2 = jnp.concatenate([jnp.zeros_like(ydown), ydown], 0)
    yup2 = send((piece(1) + yup2.astype(F32)).astype(BF16), YUP)
    ydown2 = send((piece(3) + ydown2.astype(F32)).astype(BF16), YDOWN)
    total = piece(0) + yup2.astype(F32) + ydown2.astype(F32)
    left, right = total[:, :640], total[:, 640:]
    away = jnp.where(xl == 0, right, left).astype(BF16)
    d_context = jnp.where(xl == 0, left, right) + send(away, XLO).astype(F32)
    d_context = d_context.astype(BF16)

    for d in (3, 2, 1):
        if d < 3:
            up = (part(d) + up.astype(F32)).astype(BF16)
            down = (part(-d) + down.astype(F32)).astype(BF16)
        up, down = send(up, ZUP), send(down, ZDOWN)
    total = part(0) + up.astype(F32) + down.astype(F32)
    left, right = total[:, :640], total[:, 640:]
    away = jnp.where(side == 0, right, left).astype(BF16)
    total = jnp.where(side == 0, left, right) + send(away, XHI).astype(F32)
    total = total.astype(BF16)
    w_grad = send(total, BACK).astype(F32) * (1.0 / math.sqrt(TOKENS))

    kept, got = normed[:, :, :320], send(normed[:, :, 320:], CORE)
    kept = jnp.where(par == 0, kept, kept[::-1])
    got = jnp.where(par == 0, got, got[::-1])
    normed = jnp.where(
        c == 0, jnp.stack([kept, got], 1), jnp.stack([got, kept], 1)
    )
    normed = normed.reshape(640, 320).T
    return (normed, d_context, w_grad)


def solution(mesh):
    return jax.shard_map(
        per_device,
        mesh=mesh,
        in_specs=(
            P("loop", "tensor"),
            P("tensor", "loop"),
            P("loop", "tensor"),
            P(),
            P("loop", "tensor"),
        ),
        out_specs=(P("loop", "tensor"), P("loop", "tensor"), P("loop", "tensor")),
        check_vma=False,
    )
```
